512 devices in a mesh: sec: 4 (over z_hi), seq: 128 (over z_lo, x, y, core).
Axes of the slice: x: 4, y: 4, z: 16 (z_hi: 4, z_lo: 4; z = z_hi * 4 + z_lo), core: 2. Of those that a mesh axis runs over, the one named last changes fastest.
Arguments:
- video: bfloat16 [3, 128, 512, 256], P(None, 'seq', 'sec'), may hold values from -6 to 6
- conv_weight: bfloat16 [128, 81], replicated, may hold values from -0.625 to 0.625
- down_weight: bfloat16 [128, 8, 8, 16], replicated, may hold values from -0.0625 to 0.0625
- noise: bfloat16 [16, 128, 64, 32], P(None, 'seq', 'sec'), may hold values from -6 to 6
- timesteps: int32 [128], P('seq'), may hold values from 0 to 999
- embed_weight: bfloat16 [64, 3072], replicated, may hold values from -0.75 to 0.75
- mod_weight: bfloat16 [256, 3072], replicated, may hold values from -0.375 to 0.375
- qkv_weight: bfloat16 [3072, 12, 384], P('seq', 'sec'), may hold values from -0.109375 to 0.109375
- cotangent: bfloat16 [128, 512, 1536], P('seq', 'sec'), may hold values from -24 to 24
Outputs:
- latents: bfloat16 [16, 128, 64, 32], P(None, 'seq', 'sec')
- attended: bfloat16 [128, 512, 1536], P('seq', 'sec')
- out_grad: float32 [1536, 1536], P('seq', 'sec')
The draws below stay inside these ranges and needn't reach their ends.
All inputs are finite; a program needn't handle non-finite values.
Results may differ from the reference program's by a relative error of at most 0.01.
Values may be sent and summed in bfloat16 or wider, within the bound.
No kernel may reach another device: no remote copies, remote signals or barrier semaphores. Data moves between devices by JAX's collectives and lax.ppermute only.
A program may use at most 128 MiB of HBM per device.

```python
import math
import jax
import jax.numpy as jnp
from jax import lax

CH_IN = 3
ENC_CH = 128
LAT = 16
ROWS = 512
WIDTH = 256
D = 3072
HEADS = 12
HD = 128
DOUT = 1536
TEMB = 256
STEPS = 1000
FRAMES = 128
BAND = 128
TOKF = 512
N_SEC = 4


def place_ends(entries, stream_key, smallest, top_value):
    longest = entries.shape.index(max(entries.shape))
    spots = []
    for shift in (0, 1):
        where = [jax.random.randint(jax.random.fold_in(stream_key, axis), (), 0, length) for axis, length in enumerate(entries.shape)]
        where[longest] = (where[longest] + shift) % entries.shape[longest]
        spots.append(tuple(where))
    return entries.at[spots[0]].set(smallest).at[spots[1]].set(top_value)


def strengthened(result, key, source, target, parts, factor):
    def block_of(dim):
        return (jnp.arange(result.shape[dim]) // (result.shape[dim] // parts)).reshape((-1,) + (1,) * (result.ndim - 1 - dim))

    one_side = jax.random.permutation(key, parts)[block_of(target)]
    far = (block_of(target) + parts // 2) % parts
    return jnp.where((block_of(source) == one_side) | (block_of(source) == far), factor * result, result)


def shard_levels(own_key, shape, shards, smallest, high):
    level = 1.0
    for position, parts in shards:
        draws = jax.random.uniform(jax.random.fold_in(jax.random.fold_in(own_key, 6), position), (parts,), jnp.float32, smallest / len(shards), high / len(shards))
        level = level * jnp.repeat(jnp.exp(draws), shape[position] // parts).reshape((-1,) + (1,) * (len(shape) - 1 - position))
    return level


def normal_values(stream_key, dims, scale, bound, shards=(), kind=jnp.bfloat16):
    level = shard_levels(stream_key, dims, shards, -0.22, 0.18) if shards else 1.0
    result = jax.random.normal(stream_key, dims, jnp.float32) * scale * level
    return jnp.minimum(jnp.maximum(result, -bound), bound).astype(kind)


def bell_draw_with(key, shape, scale, most, split, heavy, kind=jnp.bfloat16):
    array = scale * jax.random.normal(key, shape, jnp.float32)
    if split:
        array = array * shard_levels(key, shape, split, -0.22, 0.18)
    return jnp.clip(strengthened(array, jax.random.fold_in(key, 3), *heavy), -most, most).astype(kind)


def setup_inputs(seed: int = 0) -> dict:
    keys = jax.random.split(jax.random.key(seed), 10)
    video = normal_values(keys[0], (CH_IN, FRAMES, ROWS, WIDTH), 1.0, 6.0, ((1, 128), (2, 4)))
    conv_weight = normal_values(keys[1], (ENC_CH, CH_IN * 27), (CH_IN * 27) ** -0.5, 0.625)
    down_weight = normal_values(keys[2], (ENC_CH, 8, 8, LAT), (ENC_CH * 64) ** -0.5, 0.0625)
    noise = normal_values(keys[3], (LAT, FRAMES, ROWS // 8, WIDTH // 8), 1.0, 6.0, ((1, 128), (2, 4)))
    timesteps = place_ends(jax.random.randint(keys[4], (FRAMES,), 0, STEPS), jax.random.fold_in(keys[4], 1), 0, STEPS - 1).astype(jnp.int32)
    embed_weight = normal_values(keys[5], (LAT * 4, D), (LAT * 4) ** -0.5, 0.75)
    mod_weight = normal_values(keys[6], (TEMB, D), TEMB ** -0.5, 0.375)
    qkv_weight = normal_values(keys[7], (D, HEADS, 3 * HD), D ** -0.5, 0.109375, ((0, 128), (1, 4)))
    cotangent = bell_draw_with(keys[8], (FRAMES, TOKF, DOUT), 1.0, 24.0, ((0, 128), (1, 4)), (0, 2, 128, 5.5))
    return {"video": video, "conv_weight": conv_weight, "down_weight": down_weight, "noise": noise, "timesteps": timesteps, "embed_weight": embed_weight, "mod_weight": mod_weight, "qkv_weight": qkv_weight, "cotangent": cotangent}


def encode_rows(pixels, conv_weight, down_weight):
    channels = pixels.shape[0]
    height = pixels.shape[2] - 2
    breadth = pixels.shape[3] - 2
    windows = []
    for channel in range(channels):
        for shift_t in range(3):
            for shift_y in range(3):
                for shift_x in range(3):
                    windows.append(pixels[channel, shift_t, shift_y:shift_y + height, shift_x:shift_x + breadth])
    columns = jnp.stack(windows).reshape(len(windows), height * breadth)
    before = jnp.dot(conv_weight, columns, preferred_element_type=jnp.float32)
    feature = jax.nn.silu(before).astype(jnp.bfloat16)
    feature = feature.reshape(feature.shape[0], height // 8, 8, breadth // 8, 8)
    latent = jnp.einsum('caiej,cijl->lae', feature.astype(jnp.float32), down_weight.astype(jnp.float32))
    return latent.astype(jnp.bfloat16)

def noisy_latents(latents, noise, timesteps):
    noise_level = (timesteps.astype(jnp.float32) + 1.0) / STEPS
    noise_level = noise_level[None, :, None, None]
    blended = (1.0 - noise_level) * latents.astype(jnp.float32) + noise_level * noise.astype(jnp.float32)
    return blended.astype(jnp.bfloat16)

def frame_patches(noised):
    channels, lat_rows, lat_cols = noised.shape
    blocks = noised.reshape(channels, lat_rows // 2, 2, lat_cols // 2, 2).transpose(1, 3, 0, 2, 4)
    return blocks.reshape(lat_rows // 2 * (lat_cols // 2), channels * 4)

def modulation(timesteps, mod_weight):
    half_width = mod_weight.shape[0] // 2
    frequency = jnp.exp(-math.log(10000.0) * jnp.arange(half_width, dtype=jnp.float32) / half_width)
    angles = timesteps.astype(jnp.float32)[:, None] * frequency[None, :]
    embedded = jnp.concatenate([jnp.cos(angles), jnp.sin(angles)], axis=1)
    return jnp.dot(embedded, mod_weight.astype(jnp.float32), precision=lax.Precision.HIGHEST)

def prepare(patches, embed_weight, mod_scale):
    embedded = jnp.dot(patches, embed_weight, preferred_element_type=jnp.float32)
    center = embedded - lax.optimization_barrier(jnp.mean(embedded, axis=1, keepdims=True))
    spread = lax.optimization_barrier(jnp.mean(center * center, axis=1, keepdims=True))
    normed = center * lax.rsqrt(spread + 1e-06) * (1.0 + mod_scale)
    return normed.astype(jnp.bfloat16)

def attention(projected):
    head_size = projected.shape[3]
    queries = projected[:, :, 0].astype(jnp.float32)
    key_rows = projected[:, :, 1].astype(jnp.float32)
    values = projected[:, :, 2].astype(jnp.float32)
    scores = jnp.einsum('qhd,khd->hqk', queries, key_rows) / math.sqrt(head_size)
    attn_probs = jax.nn.softmax(scores, axis=-1).astype(jnp.bfloat16)
    output = jnp.einsum('hqk,khd->qhd', attn_probs.astype(jnp.float32), values)
    return output.astype(jnp.bfloat16).reshape(projected.shape[0], projected.shape[1] * head_size)

def reference(video, conv_weight, down_weight, noise, timesteps, embed_weight, mod_weight, qkv_weight, cotangent):
    padded = jnp.pad(video, ((0, 0), (2, 0), (1, 1), (1, 1)))

    def one_frame(frame_index):
        window = lax.dynamic_slice_in_dim(padded, frame_index, 3, 1)

        def one_band(band_index):
            pixels = lax.dynamic_slice_in_dim(window, band_index * BAND, BAND + 2, 2)
            return encode_rows(pixels, conv_weight, down_weight)
        band_list = lax.map(one_band, jnp.arange(N_SEC, dtype=jnp.int32))
        return band_list.transpose(1, 0, 2, 3).reshape(LAT, ROWS // 8, WIDTH // 8)
    latents = lax.map(one_frame, jnp.arange(FRAMES, dtype=jnp.int32)).transpose(1, 0, 2, 3)
    noised = noisy_latents(latents, noise, timesteps)
    patches = jax.vmap(frame_patches)(noised.transpose(1, 0, 2, 3))
    mod_scale = modulation(timesteps, mod_weight)
    weight_flat = qkv_weight.reshape(D, HEADS * 3 * HD)

    def frame_step(running, inputs):
        one_patches, one_scale, one_grads = inputs
        normed = prepare(one_patches, embed_weight, one_scale[None, :])
        projected = jnp.dot(normed, weight_flat, preferred_element_type=jnp.float32).astype(jnp.bfloat16)
        attended = attention(projected.reshape(TOKF, HEADS, 3, HD))
        running = running + lax.dot_general(one_grads, attended, (((0,), (0,)), ((), ())), preferred_element_type=jnp.float32)
        return (running, attended)
    start_total = jnp.zeros((DOUT, HEADS * HD), jnp.float32)
    out_grad, attended_all = lax.scan(frame_step, start_total, (patches, mod_scale, cotangent))
    return (latents, attended_all, out_grad)
```

```python
import math

import jax
import jax.numpy as jnp
from jax import lax
from jax.experimental import pallas as pl
from jax.experimental.pallas import tpu as pltpu
from jax.sharding import Mesh, PartitionSpec as P

STEPS = 1000
SEQ = ("zl", "x", "y", "core")
F32 = jnp.float32
BF16 = jnp.bfloat16
VMEM = pl.BlockSpec(memory_space=pltpu.VMEM)
SMEM = pl.BlockSpec(memory_space=pltpu.SMEM)
VMEM_BYTES = 48 * 1024 * 1024


def call(body, out_shape, n_smem, n_vmem, flops, nbytes, scratch=()):
    several = isinstance(out_shape, (list, tuple))
    return pl.pallas_call(
        body,
        out_shape=out_shape,
        in_specs=[SMEM] * n_smem + [VMEM] * n_vmem,
        out_specs=[VMEM] * len(out_shape) if several else VMEM,
        scratch_shapes=list(scratch),
        compiler_params=pltpu.CompilerParams(vmem_limit_bytes=VMEM_BYTES),
        cost_estimate=pl.CostEstimate(flops=flops, bytes_accessed=nbytes, transcendentals=0),
    )


def iota(shape, dim):
    return lax.broadcasted_iota(jnp.int32, shape, dim)


def one_hot(where):
    return jnp.where(where, 1.0, 0.0).astype(BF16)


def prep_body(place, embed, mod, temb, a_hi, a_lo, gram):
    core = place[0]
    start = pl.multiple_of(place[1] * 768, 128)
    to, of = iota((64, 64), 0), iota((64, 64), 1)
    order = one_hot(of == (to & 15) * 4 + ((to >> 4) & 1) * 2 + (to >> 5))
    emb = jnp.dot(order, embed[...], preferred_element_type=F32)
    mean = jnp.mean(emb, axis=1, keepdims=True)
    center = emb - mean
    gram[...] = (
        lax.dot_general(
            center,
            center,
            (((1,), (1,)), ((), ())),
            precision=lax.Precision.HIGHEST,
            preferred_element_type=F32,
        )
        / embed.shape[1]
    )
    col = iota((768, 384), 1)
    block = (col * 2731) >> 16
    pick = one_hot(iota((768, 384), 0) == 24 * block + 24 * core + col)
    emb_part = jnp.dot(order, embed[:, pl.ds(start, 768)], preferred_element_type=F32)
    emb_pick = jnp.dot(emb_part.astype(BF16), pick, preferred_element_type=F32) - mean
    mod_pick = jnp.dot(mod[:, pl.ds(start, 768)], pick, preferred_element_type=F32).astype(BF16)
    t = temb[...]
    first = t.astype(BF16).astype(F32)
    second = (t - first).astype(BF16).astype(F32)
    third = t - first - second
    pieces = jnp.concatenate([first, second, third], axis=0).astype(BF16)
    scale = jnp.dot(pieces, mod_pick, preferred_element_type=F32)
    scale = 1.0 + (scale[0:8] + scale[8:16] + scale[16:24])
    for f in range(8):
        a = emb_pick * scale[f : f + 1]
        hi = a.astype(BF16)
        a_hi[64 * f : 64 * f + 64] = hi
        a_lo[64 * f : 64 * f + 64] = (a - hi.astype(F32)).astype(BF16)


def fold_body(a_hi, a_lo, w, keep, send):
    for h in range(3):
        for out, rows in ((send, slice(256, 512)), (keep, slice(0, 256))):
            out[:, 384 * h : 384 * h + 384] = jnp.dot(
                a_hi[rows], w[h], preferred_element_type=F32
            ) + jnp.dot(a_lo[rows], w[h], preferred_element_type=F32)


def encode_body(level, v2, v1, v0, conv, down, noise, lat, pat, s32, s16, rows_out):
    x = iota((136, 256), 1)
    for c in range(3):
        for dt, v in enumerate((v2, v1, v0)):
            img = v[c, 0].astype(F32)
            left = jnp.where(x[:130] == 0, 0.0, pltpu.roll(img, 1, 1))
            right = jnp.where(x[:130] == 255, 0.0, pltpu.roll(img, 255, 1))
            for dx, shifted in enumerate((left, img, right)):
                k = dx * 9 + c * 3 + dt
                for half in range(2):
                    part = shifted[:, 128 * half : 128 * half + 128]
                    s32[half, pl.ds(32 + k, 128, stride=32), :] = part[0:128]
                    s32[half, pl.ds(129 * 32 + k, 1), :] = part[128:129]
                    s32[half, pl.ds(k, 1), :] = part[129:130]
    for k in range(27, 32):
        for half in range(2):
            s32[half, pl.ds(k, 130, stride=32), :] = jnp.zeros((130, 128), F32)

    def pack(i, _):
        rows = pl.ds(pl.multiple_of(i * 320, 64), 320)
        for half in range(2):
            s16[rows, 128 * half : 128 * half + 128] = s32[half, rows, :].astype(BF16)
        return 0

    lax.fori_loop(0, 13, pack, 0)
    own_lane = (iota((128, 256), 1) & 7) == (iota((128, 256), 0) >> 4)

    def block_row(a, _):
        feats = []
        for q in range(4):
            taps = s16[pl.ds(pl.multiple_of(a * 256 + 64 * q, 64), 128), :]
            pre = jnp.dot(conv[...], taps, preferred_element_type=F32)
            half = 0.5 * pre
            feats.append((half + half * jnp.tanh(half)).astype(BF16))
        feature = jnp.concatenate(feats, axis=0)
        weights = jnp.concatenate([down[i] for i in range(8)], axis=1)
        prod = jnp.dot(weights, feature, preferred_element_type=F32)
        prod = jnp.where(own_lane, prod, 0.0)
        acc = prod[0:16]
        for j in range(1, 8):
            acc = acc + prod[16 * j : 16 * j + 16]
        for by in (1, 2, 4):
            acc = acc + pltpu.roll(acc, 256 - by, 1)
        rows_out[pl.ds(pl.multiple_of(a * 16, 16), 16), :] = acc.astype(BF16)
        return 0

    lax.fori_loop(0, 16, block_row, 0)
    pick = one_hot(iota((256, 32), 0) == 8 * iota((256, 32), 1))
    lat[...] = jnp.dot(rows_out[...], pick, preferred_element_type=F32).astype(BF16)
    px, tok = iota((256, 128), 0), iota((256, 128), 1)
    for w in range(2):
        acc = jnp.zeros((32, 128), F32)
        for r in range(8):
            place = one_hot((px == 16 * (tok & 15) + 8 * w) & ((tok >> 4) == r))
            acc = acc + jnp.dot(
                rows_out[32 * r : 32 * r + 32], place, preferred_element_type=F32
            )
        t = level[0]
        mixed = (1.0 - t) * acc + t * noise[32 * w : 32 * w + 32].astype(F32)
        pat[32 * w : 32 * w + 32] = mixed.astype(BF16)


def attend_body(pats, parts, gram, att):
    tokens_t = jnp.concatenate([pats[s] for s in range(4)], axis=1).astype(F32)
    tokens = tokens_t.T
    spread = jnp.sum(
        tokens
        * jnp.dot(
            tokens, gram[...], precision=lax.Precision.HIGHEST, preferred_element_type=F32
        ),
        axis=1,
        keepdims=True,
    )
    scale = lax.rsqrt(spread + 1e-06)
    total = (parts[0].astype(F32) + parts[1].astype(F32)) + (
        parts[2].astype(F32) + parts[3].astype(F32)
    )
    hi = total.astype(BF16)
    lo = (total - hi.astype(F32)).astype(BF16)
    weights = jnp.concatenate([hi, lo], axis=0)
    twice = jnp.concatenate([tokens, tokens], axis=1).astype(BF16)
    for h in range(3):
        proj = jnp.dot(
            twice, weights[:, 384 * h : 384 * h + 384], preferred_element_type=F32
        )
        proj = (proj * scale).astype(BF16)
        q, k, v = proj[:, 0:128], proj[:, 128:256], proj[:, 256:384]
        scores = lax.dot_general(
            q, k, (((1,), (1,)), ((), ())), preferred_element_type=F32
        ) * (1.0 / math.sqrt(128.0))
        probs = jnp.exp(scores - jnp.max(scores, axis=1, keepdims=True))
        norm = 1.0 / jnp.sum(probs, axis=1, keepdims=True)
        out = jnp.dot(probs.astype(BF16), v, preferred_element_type=F32) * norm
        att[:, 128 * h : 128 * h + 128] = out.astype(BF16)


def grad_body(place, att, c0, c_up, c_down, far_a, far_b, out, full, blocks):
    s = place[0]
    sides = []
    for step in (0, 3, 1, 2):
        row = pl.multiple_of(lax.rem(s + step, 4) * 128, 128)
        sides.append(att[pl.ds(row, 128), :])
    rhs = jnp.concatenate(sides, axis=0)
    for half, far in enumerate((far_a, far_b)):
        rows = slice(768 * half, 768 * half + 768)
        lhs = jnp.concatenate([c0[rows], c_up[rows], c_down[rows], far[...]], axis=1)
        full[rows] = jnp.dot(lhs, rhs, preferred_element_type=F32)
    for d in range(32):
        for z in range(4):
            blocks[48 * d + 12 * z : 48 * d + 12 * z + 12] = full[
                384 * z + 12 * d : 384 * z + 12 * d + 12
            ]
        out[d] = blocks[48 * d : 48 * d + 48].astype(BF16)


def moved(shard, axis, size, by, wrap):
    pairs = [(i, (i + by) % size) for i in range(size) if wrap or 0 <= i + by < size]
    return lax.ppermute(shard, axis, pairs)


def on_device(
    video,
    conv_weight,
    down_weight,
    noise,
    timesteps,
    embed_weight,
    mod_weight,
    qkv_weight,
    cotangent,
):
    core, zl, sec = lax.axis_index("core"), lax.axis_index("zl"), lax.axis_index("sec")
    above = moved(video[:, :, 127:128], "sec", 4, 1, False)
    below = moved(video[:, :, 0:1], "sec", 4, -1, False)
    v0 = jnp.concatenate([video, below, above], axis=2)
    v1 = moved(v0, SEQ, 128, 1, False)
    v2 = moved(v0, SEQ, 128, 2, False)

    cot = cotangent[0].T
    c_up = moved(cot, "sec", 4, 1, True)
    c_down = moved(cot, "sec", 4, -1, True)
    far_a = moved(c_up[0:768], "sec", 4, 1, True)
    far_b = moved(c_down[768:1536], "sec", 4, -1, True)

    stamps = lax.all_gather(timesteps, ("zl", "core"), axis=0, tiled=True).reshape(4, 2)
    mine = lax.dynamic_index_in_dim(stamps, core, 1, keepdims=False)
    theirs = lax.dynamic_index_in_dim(stamps, 1 - core, 1, keepdims=False)
    stamps = jnp.concatenate([mine, theirs])
    frequency = jnp.exp(-math.log(10000.0) * jnp.arange(128, dtype=F32) / 128)
    angles = stamps.astype(F32)[:, None] * frequency[None, :]
    temb = jnp.concatenate([jnp.cos(angles), jnp.sin(angles)], axis=1)
    place = jnp.stack([core, zl]).astype(jnp.int32)
    a_hi, a_lo, gram = call(
        prep_body,
        [
            jax.ShapeDtypeStruct((512, 384), BF16),
            jax.ShapeDtypeStruct((512, 384), BF16),
            jax.ShapeDtypeStruct((64, 64), F32),
        ],
        1,
        3,
        10**9,
        3 * 10**6,
    )(place, embed_weight, mod_weight, temb)
    rows = lax.all_gather(qkv_weight, ("x", "y"), axis=0, tiled=True)
    keep, send = call(
        fold_body,
        [jax.ShapeDtypeStruct((256, 1152), F32)] * 2,
        0,
        3,
        10**9,
        5 * 10**6,
    )(a_hi, a_lo, rows.transpose(1, 0, 2))
    pair = (keep + moved(send, "core", 2, 1, True)).astype(BF16).reshape(4, 64, 1152)
    parts = lax.all_to_all(pair, "zl", 0, 0, tiled=True)

    taps = conv_weight.reshape(128, 3, 3, 3, 3).transpose(0, 3, 4, 1, 2).reshape(128, 3, 27)
    taps = jnp.pad(taps, ((0, 0), (0, 0), (0, 5))).reshape(128, 96)
    conv = jnp.concatenate(
        [jnp.pad(taps, ((0, 0), (0, 32))), jnp.pad(taps, ((0, 0), (32, 0)))], axis=0
    )
    down = down_weight.transpose(1, 2, 3, 0).reshape(8, 128, 128)
    noise_t = noise.reshape(16, 8, 2, 16, 2).transpose(4, 2, 0, 1, 3).reshape(64, 128)
    level = (timesteps.astype(F32) + 1.0) / STEPS
    lat, pat = call(
        encode_body,
        [jax.ShapeDtypeStruct((256, 32), BF16), jax.ShapeDtypeStruct((64, 128), BF16)],
        1,
        6,
        10**10,
        10**6,
        [
            pltpu.VMEM((2, 4160, 128), F32),
            pltpu.VMEM((4160, 256), BF16),
            pltpu.VMEM((256, 256), BF16),
        ],
    )(level, v2, v1, v0, conv, down, noise_t)
    latents = lat.reshape(16, 16, 32).transpose(1, 0, 2)[:, None]

    pats = lax.all_gather(pat, "sec", axis=0)
    att = call(
        attend_body, jax.ShapeDtypeStruct((512, 384), BF16), 0, 3, 4 * 10**9, 10**6
    )(pats, parts, gram)
    attended = lax.all_to_all(att, "sec", split_axis=0, concat_axis=1, tiled=True)

    blocks = call(
        grad_body,
        jax.ShapeDtypeStruct((32, 48, 384), BF16),
        1,
        6,
        10**9,
        5 * 10**6,
        [pltpu.VMEM((1536, 384), F32), pltpu.VMEM((1536, 384), F32)],
    )(sec.astype(jnp.int32)[None], att, cot, c_up, c_down, far_a, far_b)
    got = lax.all_to_all(blocks, ("x", "y", "core"), 0, 0, tiled=True)
    summed = jnp.sum(got.astype(F32), axis=0).astype(BF16).reshape(4, 12, 384)
    last = lax.all_to_all(summed, "zl", 0, 0, tiled=True)
    out_grad = jnp.sum(last.astype(F32), axis=0)
    return (latents, attended[None], out_grad)


def solution(mesh):
    split = Mesh(mesh.devices.reshape(4, 4, 4, 4, 2), ("sec",) + SEQ)
    in_specs = (
        P(None, SEQ, "sec", None),
        P(),
        P(),
        P(None, SEQ, "sec", None),
        P(SEQ),
        P(),
        P(),
        P(SEQ, "sec", None),
        P(SEQ, "sec", None),
    )
    out_specs = (P(None, SEQ, "sec", None), P(SEQ, "sec", None), P(SEQ, "sec"))
    return jax.shard_map(
        on_device, mesh=split, in_specs=in_specs, out_specs=out_specs, check_vma=False
    )
```

```python
import math

import jax
import jax.numpy as jnp
from jax import lax
from jax.experimental import pallas as pl
from jax.experimental.pallas import tpu as pltpu
from jax.sharding import Mesh, PartitionSpec as P

STEPS = 1000
SEQ = ("zl", "x", "y", "core")
F32 = jnp.float32
BF16 = jnp.bfloat16
VMEM = pl.BlockSpec(memory_space=pltpu.VMEM)
SMEM = pl.BlockSpec(memory_space=pltpu.SMEM)
ANY = pl.BlockSpec(memory_space=pl.ANY)
VMEM_BYTES = 48 * 1024 * 1024


def call(body, out_shape, n_smem, n_vmem, flops, nbytes, scratch=(), n_any=0):
    several = isinstance(out_shape, (list, tuple))
    return pl.pallas_call(
        body,
        out_shape=out_shape,
        in_specs=[SMEM] * n_smem + [VMEM] * n_vmem + [ANY] * n_any,
        out_specs=[VMEM] * len(out_shape) if several else VMEM,
        scratch_shapes=list(scratch),
        compiler_params=pltpu.CompilerParams(vmem_limit_bytes=VMEM_BYTES),
        cost_estimate=pl.CostEstimate(flops=flops, bytes_accessed=nbytes, transcendentals=0),
    )


def iota(shape, dim):
    return lax.broadcasted_iota(jnp.int32, shape, dim)


def one_hot(where):
    return jnp.where(where, 1.0, 0.0).astype(BF16)


def prep_body(place, embed, mod, temb, a_hi, a_lo, gram):
    to, of = iota((64, 64), 0), iota((64, 64), 1)
    order = one_hot(of == (to & 15) * 4 + ((to >> 4) & 1) * 2 + (to >> 5))
    emb = jnp.dot(order, embed[...], preferred_element_type=F32)
    mean = jnp.mean(emb, axis=1, keepdims=True)
    center = emb - mean
    gram[...] = (
        lax.dot_general(
            center,
            center,
            (((1,), (1,)), ((), ())),
            precision=lax.Precision.HIGHEST,
            preferred_element_type=F32,
        )
        / embed.shape[1]
    )
    col = iota((768, 192), 1)
    part = (col * 1366) >> 16
    hit = iota((768, 192), 0) == 48 * place[0] + col - 48 * part
    emb16 = emb.astype(BF16)
    emb_pick = jnp.zeros((64, 192), F32)
    mod_pick = jnp.zeros((256, 192), F32)
    for z in range(4):
        pick = one_hot(hit & (part == z))
        at = slice(768 * z, 768 * z + 768)
        emb_pick = emb_pick + jnp.dot(emb16[:, at], pick, preferred_element_type=F32)
        mod_pick = mod_pick + jnp.dot(mod[:, at], pick, preferred_element_type=F32)
    emb_pick = emb_pick - mean
    t = temb[...]
    first = t.astype(BF16).astype(F32)
    second = (t - first).astype(BF16).astype(F32)
    third = t - first - second
    pieces = jnp.concatenate([first, second, third], axis=0).astype(BF16)
    scale = jnp.dot(pieces, mod_pick.astype(BF16), preferred_element_type=F32)
    scale = 1.0 + (scale[0:16] + scale[16:32] + scale[32:48])
    for f in range(16):
        a = emb_pick * scale[f : f + 1]
        hi = a.astype(BF16)
        a_hi[64 * f : 64 * f + 64] = hi
        a_lo[64 * f : 64 * f + 64] = (a - hi.astype(F32)).astype(BF16)


def fold_body(a_hi, a_lo, w, out):
    for h in range(3):
        prod = jnp.dot(a_hi[...], w[h], preferred_element_type=F32) + jnp.dot(
            a_lo[...], w[h], preferred_element_type=F32
        )
        out[:, 384 * h : 384 * h + 384] = prod.astype(BF16)


def encode_body(
    level, v2, v1, v0, conv, down, noise, lat, pat, s32, edge, s16, rows_out
):
    x = iota((136, 256), 1)
    for c in range(3):
        for dt, v in enumerate((v2, v1, v0)):
            img = v[c, 0].astype(F32)
            left = jnp.where(x[:130] == 0, 0.0, pltpu.roll(img, 1, 1))
            right = jnp.where(x[:130] == 255, 0.0, pltpu.roll(img, 255, 1))
            for dx, shifted in enumerate((left, img, right)):
                k = dx * 9 + c * 3 + dt
                s32[k] = shifted[0:128]
                edge[k : k + 1] = shifted[128:129]
                edge[32 + k : 33 + k] = shifted[129:130]
    s32[27:32] = jnp.zeros((5, 128, 256), F32)
    edge[27:32] = jnp.zeros((5, 256), F32)
    edge[59:64] = jnp.zeros((5, 256), F32)
    s16[0:32] = edge[0:32].astype(BF16)
    s16[4128:4160] = edge[32:64].astype(BF16)
    for y in range(0, 128, 8):
        taps = jnp.swapaxes(s32[:, y : y + 8, :], 0, 1).reshape(256, 256)
        s16[32 * y + 32 : 32 * y + 288] = taps.astype(BF16)
    own_lane = (iota((128, 256), 1) & 7) == (iota((128, 256), 0) >> 4)

    def block_row(a, _):
        feats = []
        for q in range(4):
            taps = s16[pl.ds(pl.multiple_of(a * 256 + 64 * q, 64), 128), :]
            pre = jnp.dot(conv[...], taps, preferred_element_type=F32)
            half = 0.5 * pre
            feats.append((half + half * jnp.tanh(half)).astype(BF16))
        feature = jnp.concatenate(feats, axis=0)
        weights = jnp.concatenate([down[i] for i in range(8)], axis=1)
        prod = jnp.dot(weights, feature, preferred_element_type=F32)
        prod = jnp.where(own_lane, prod, 0.0)
        acc = prod[0:16]
        for j in range(1, 8):
            acc = acc + prod[16 * j : 16 * j + 16]
        for by in (1, 2, 4):
            acc = acc + pltpu.roll(acc, 256 - by, 1)
        rows_out[pl.ds(pl.multiple_of(a * 16, 16), 16), :] = acc.astype(BF16)
        return 0

    lax.fori_loop(0, 16, block_row, 0, unroll=True)
    pick = one_hot(iota((256, 32), 0) == 8 * iota((256, 32), 1))
    lat[...] = jnp.dot(rows_out[...], pick, preferred_element_type=F32).astype(BF16)
    px, tok = iota((256, 128), 0), iota((256, 128), 1)
    for w in range(2):
        acc = jnp.zeros((32, 128), F32)
        for r in range(8):
            place = one_hot((px == 16 * (tok & 15) + 8 * w) & ((tok >> 4) == r))
            acc = acc + jnp.dot(
                rows_out[32 * r : 32 * r + 32], place, preferred_element_type=F32
            )
        t = level[0]
        mixed = (1.0 - t) * acc + t * noise[32 * w : 32 * w + 32].astype(F32)
        pat[32 * w : 32 * w + 32] = mixed.astype(BF16)


def attend_body(pats, parts, gram, att):
    tokens_t = jnp.concatenate([pats[s] for s in range(4)], axis=1).astype(F32)
    tokens = tokens_t.T
    spread = jnp.sum(
        tokens
        * jnp.dot(
            tokens, gram[...], precision=lax.Precision.HIGHEST, preferred_element_type=F32
        ),
        axis=1,
        keepdims=True,
    )
    scale = lax.rsqrt(spread + 1e-06)
    total = parts[0].astype(F32)
    for i in range(1, 16):
        total = total + parts[i].astype(F32)
    hi = total.astype(BF16)
    lo = (total - hi.astype(F32)).astype(BF16)
    weights = jnp.concatenate([hi, lo], axis=0)
    twice = jnp.concatenate([tokens, tokens], axis=1).astype(BF16)
    for h in range(3):
        proj = jnp.dot(
            twice, weights[:, 384 * h : 384 * h + 384], preferred_element_type=F32
        )
        proj = (proj * scale).astype(BF16)
        q, k, v = proj[:, 0:128], proj[:, 128:256], proj[:, 256:384]
        scores = lax.dot_general(
            q, k, (((1,), (1,)), ((), ())), preferred_element_type=F32
        ) * (1.0 / math.sqrt(128.0))
        probs = jnp.exp(scores - jnp.max(scores, axis=1, keepdims=True))
        norm = 1.0 / jnp.sum(probs, axis=1, keepdims=True)
        out = jnp.dot(probs.astype(BF16), v, preferred_element_type=F32) * norm
        att[:, 128 * h : 128 * h + 128] = out.astype(BF16)


def grad_body(place, att, c0, c_up, c_down, far_a, far_b, out0, out1, out2, out3, full):
    sec, y = place[0], place[1]
    sides = []
    for step in (0, 3, 1, 2):
        row = pl.multiple_of(((sec + step) & 3) * 128, 128)
        sides.append(att[pl.ds(row, 128), :])
    rhs = jnp.concatenate(sides, axis=0)
    for half, far in enumerate((far_a, far_b)):
        rows = slice(768 * half, 768 * half + 768)
        lhs = jnp.concatenate([c0[rows], c_up[rows], c_down[rows], far[...]], axis=1)
        full[rows] = jnp.dot(lhs, rhs, preferred_element_type=F32)
    for by, out in enumerate((out0, out1, out2, out3)):
        to_y = (y + by) & 3
        for zx in range(0, 16, 2):
            pair = [
                full[pl.ds(pl.multiple_of(24 * to_y + 96 * k, 8), 24), :] for k in (zx, zx + 1)
            ]
            out[24 * zx : 24 * zx + 48] = jnp.concatenate(pair, axis=0).astype(BF16)


def gate_body(value, *rest):
    rest[-1][...] = value[...]


def gated(value, *deps):
    return pl.pallas_call(
        gate_body,
        out_shape=jax.ShapeDtypeStruct(value.shape, value.dtype),
        in_specs=[VMEM] + [ANY] * len(deps),
        out_specs=VMEM,
    )(value, *deps)


def together(*values):
    return lax.optimization_barrier(values)


def moved(shard, axis, size, by, wrap):
    pairs = [(i, (i + by) % size) for i in range(size) if wrap or 0 <= i + by < size]
    return lax.ppermute(shard, axis, pairs)


def on_device(
    video,
    conv_weight,
    down_weight,
    noise,
    timesteps,
    embed_weight,
    mod_weight,
    qkv_weight,
    cotangent,
):
    above = moved(video[:, :, 127:128], ("sec",), 4, 1, False)
    below = moved(video[:, :, 0:1], ("sec",), 4, -1, False)
    v0 = jnp.concatenate([video, above, below], axis=2)
    v1, v2 = moved(v0, SEQ, 128, 1, False), moved(v0, SEQ, 128, 2, False)

    rows = lax.all_to_all(
        jnp.broadcast_to(qkv_weight.transpose(1, 0, 2), (8, 3, 24, 384)), ("zl", "core"), 0, 0, tiled=True
    )
    rows = rows.transpose(1, 0, 2, 3).reshape(3, 192, 384)
    stamps = lax.all_gather(gated(timesteps, v1, v2), ("x", "y"), axis=0, tiled=True)

    cot = gated(cotangent[0].T, above, below)
    c_up = moved(cot, "sec", 4, 1, True)
    c_down = moved(cot, "sec", 4, -1, True)

    frequency = jnp.exp(-math.log(10000.0) * jnp.arange(128, dtype=F32) / 128)
    angles = stamps.astype(F32)[:, None] * frequency[None, :]
    temb = jnp.concatenate([jnp.cos(angles), jnp.sin(angles)], axis=1)
    place = (lax.axis_index("x") * 4 + lax.axis_index("y")).astype(jnp.int32)[None]
    a_hi, a_lo, gram = call(
        prep_body,
        [
            jax.ShapeDtypeStruct((1024, 192), BF16),
            jax.ShapeDtypeStruct((1024, 192), BF16),
            jax.ShapeDtypeStruct((64, 64), F32),
        ],
        1,
        3,
        10**9,
        3 * 10**6,
    )(place, embed_weight, mod_weight, temb)
    partial = call(
        fold_body, jax.ShapeDtypeStruct((1024, 1152), BF16), 0, 3, 10**9, 5 * 10**6
    )(a_hi, a_lo, rows)
    taps = conv_weight.reshape(128, 3, 3, 3, 3).transpose(0, 3, 4, 1, 2).reshape(128, 3, 27)
    taps = jnp.pad(taps, ((0, 0), (0, 0), (0, 5))).reshape(128, 96)
    conv = jnp.concatenate(
        [jnp.pad(taps, ((0, 0), (0, 32))), jnp.pad(taps, ((0, 0), (32, 0)))], axis=0
    )
    down = down_weight.transpose(1, 2, 3, 0).reshape(8, 128, 128)
    noise_t = noise.reshape(16, 8, 2, 16, 2).transpose(4, 2, 0, 1, 3).reshape(64, 128)
    level = (timesteps.astype(F32) + 1.0) / STEPS
    lat, pat = call(
        encode_body,
        [jax.ShapeDtypeStruct((256, 32), BF16), jax.ShapeDtypeStruct((64, 128), BF16)],
        1,
        6,
        10**10,
        10**6,
        [
            pltpu.VMEM((32, 128, 256), F32),
            pltpu.VMEM((64, 256), F32),
            pltpu.VMEM((4160, 256), BF16),
            pltpu.VMEM((256, 256), BF16),
        ],
    )(level, v2, v1, v0, conv, down, noise_t)
    latents = lat.reshape(16, 16, 32).transpose(1, 0, 2)[:, None]

    pat, partial, c_up, c_down = together(pat, partial, c_up, c_down)
    parts = lax.all_to_all(partial.reshape(16, 64, 1152), ("x", "y"), 0, 0, tiled=True)
    pats = lax.all_gather(pat, "sec", axis=0)
    pats, c_up, c_down = together(pats, c_up, c_down)
    far_a = moved(c_up[0:768], "sec", 4, 1, True)
    far_b = moved(c_down[768:1536], "sec", 4, -1, True)
    parts, far_a, far_b = together(parts, far_a, far_b)
    att = call(
        attend_body, jax.ShapeDtypeStruct((512, 384), BF16), 0, 3, 4 * 10**9, 10**6
    )(pats, parts, gram)
    attended = lax.all_to_all(att, "sec", split_axis=0, concat_axis=1, tiled=True)

    sums = call(
        grad_body,
        [jax.ShapeDtypeStruct((384, 384), BF16)] * 4,
        1,
        6,
        10**9,
        5 * 10**6,
        [pltpu.VMEM((1536, 384), F32)],
    )(
        jnp.stack([lax.axis_index("sec"), lax.axis_index("y")]).astype(jnp.int32),
        att,
        cot,
        c_up,
        c_down,
        far_a,
        far_b,
    )
    got = [moved(sums[by], "y", 4, by, True).astype(F32) for by in range(1, 4)]
    column = sum(got, sums[0].astype(F32)).astype(BF16).reshape(32, 12, 384)
    last = lax.all_to_all(column, ("zl", "x", "core"), 0, 0, tiled=True)
    out_grad = jnp.sum(last.astype(F32), axis=0)
    return (latents, attended[None], out_grad)


def solution(mesh):
    split = Mesh(mesh.devices.reshape(4, 4, 4, 4, 2), ("sec",) + SEQ)
    in_specs = (
        P(None, SEQ, "sec", None),
        P(),
        P(),
        P(None, SEQ, "sec", None),
        P(SEQ),
        P(),
        P(),
        P(SEQ, "sec", None),
        P(SEQ, "sec", None),
    )
    out_specs = (P(None, SEQ, "sec", None), P(SEQ, "sec", None), P(SEQ, "sec"))
    return jax.shard_map(
        on_device, mesh=split, in_specs=in_specs, out_specs=out_specs, check_vma=False
    )
```

```python
import math

import jax
import jax.numpy as jnp
from jax import lax
from jax.experimental import pallas as pl
from jax.experimental.pallas import tpu as pltpu
from jax.sharding import Mesh, PartitionSpec as P

STEPS = 1000
SEQ = ("zl", "x", "y", "core")
F32 = jnp.float32
BF16 = jnp.bfloat16
VMEM = pl.BlockSpec(memory_space=pltpu.VMEM)
SMEM = pl.BlockSpec(memory_space=pltpu.SMEM)
ANY = pl.BlockSpec(memory_space=pl.ANY)
VMEM_BYTES = 48 * 1024 * 1024


def call(body, out_shape, n_smem, n_vmem, flops, nbytes, scratch=(), n_any=0):
    several = isinstance(out_shape, (list, tuple))
    return pl.pallas_call(
        body,
        out_shape=out_shape,
        in_specs=[SMEM] * n_smem + [VMEM] * n_vmem + [ANY] * n_any,
        out_specs=[VMEM] * len(out_shape) if several else VMEM,
        scratch_shapes=list(scratch),
        compiler_params=pltpu.CompilerParams(vmem_limit_bytes=VMEM_BYTES),
        cost_estimate=pl.CostEstimate(flops=flops // 10**6, bytes_accessed=nbytes // 10**5, transcendentals=0),
    )


def iota(shape, dim):
    return lax.broadcasted_iota(jnp.int32, shape, dim)


def one_hot(where):
    return jnp.where(where, 1.0, 0.0).astype(BF16)


def prep_body(place, embed, mod, temb, a_hi, a_lo, gram):
    to, of = iota((64, 64), 0), iota((64, 64), 1)
    order = one_hot(of == (to & 15) * 4 + ((to >> 4) & 1) * 2 + (to >> 5))
    emb = jnp.dot(order, embed[...], preferred_element_type=F32)
    mean = jnp.mean(emb, axis=1, keepdims=True)
    center = emb - mean
    gram[...] = (
        lax.dot_general(
            center,
            center,
            (((1,), (1,)), ((), ())),
            precision=lax.Precision.HIGHEST,
            preferred_element_type=F32,
        )
        / embed.shape[1]
    )
    col = iota((768, 192), 1)
    part = (col * 1366) >> 16
    hit = iota((768, 192), 0) == 48 * place[0] + col - 48 * part
    emb16 = emb.astype(BF16)
    emb_pick = jnp.zeros((64, 192), F32)
    mod_pick = jnp.zeros((256, 192), F32)
    for z in range(4):
        pick = one_hot(hit & (part == z))
        at = slice(768 * z, 768 * z + 768)
        emb_pick = emb_pick + jnp.dot(emb16[:, at], pick, preferred_element_type=F32)
        mod_pick = mod_pick + jnp.dot(mod[:, at], pick, preferred_element_type=F32)
    emb_pick = emb_pick - mean
    t = temb[...]
    first = t.astype(BF16).astype(F32)
    second = (t - first).astype(BF16).astype(F32)
    third = t - first - second
    pieces = jnp.concatenate([first, second, third], axis=0).astype(BF16)
    scale = jnp.dot(pieces, mod_pick.astype(BF16), preferred_element_type=F32)
    scale = 1.0 + (scale[0:16] + scale[16:32] + scale[32:48])
    for f in range(16):
        a = emb_pick * scale[f : f + 1]
        hi = a.astype(BF16)
        a_hi[64 * f : 64 * f + 64] = hi
        a_lo[64 * f : 64 * f + 64] = (a - hi.astype(F32)).astype(BF16)


def fold_body(a_hi, a_lo, w, out):
    for h in range(3):
        prod = jnp.dot(a_hi[...], w[h], preferred_element_type=F32) + jnp.dot(
            a_lo[...], w[h], preferred_element_type=F32
        )
        out[:, 384 * h : 384 * h + 384] = prod.astype(BF16)


def encode_body(
    level, v2, v1, v0, conv, down, noise, lat, pat, s32, edge, s16, rows_out
):
    x = iota((136, 256), 1)
    for c in range(3):
        for dt, v in enumerate((v2, v1, v0)):
            img = v[c, 0].astype(F32)
            left = jnp.where(x[:130] == 0, 0.0, pltpu.roll(img, 1, 1))
            right = jnp.where(x[:130] == 255, 0.0, pltpu.roll(img, 255, 1))
            for dx, shifted in enumerate((left, img, right)):
                k = dx * 9 + c * 3 + dt
                s32[k] = shifted[0:128]
                edge[k : k + 1] = shifted[128:129]
                edge[32 + k : 33 + k] = shifted[129:130]
    s32[27:32] = jnp.zeros((5, 128, 256), F32)
    edge[27:32] = jnp.zeros((5, 256), F32)
    edge[59:64] = jnp.zeros((5, 256), F32)
    s16[0:32] = edge[0:32].astype(BF16)
    s16[4128:4160] = edge[32:64].astype(BF16)
    for y in range(0, 128, 8):
        taps = jnp.swapaxes(s32[:, y : y + 8, :], 0, 1).reshape(256, 256)
        s16[32 * y + 32 : 32 * y + 288] = taps.astype(BF16)
    own_lane = (iota((128, 256), 1) & 7) == (iota((128, 256), 0) >> 4)

    def block_row(a, _):
        feats = []
        for q in range(4):
            taps = s16[pl.ds(pl.multiple_of(a * 256 + 64 * q, 64), 128), :]
            pre = jnp.dot(conv[...], taps, preferred_element_type=F32)
            half = 0.5 * pre
            feats.append((half + half * jnp.tanh(half)).astype(BF16))
        feature = jnp.concatenate(feats, axis=0)
        weights = jnp.concatenate([down[i] for i in range(8)], axis=1)
        prod = jnp.dot(weights, feature, preferred_element_type=F32)
        prod = jnp.where(own_lane, prod, 0.0)
        acc = prod[0:16]
        for j in range(1, 8):
            acc = acc + prod[16 * j : 16 * j + 16]
        for by in (1, 2, 4):
            acc = acc + pltpu.roll(acc, 256 - by, 1)
        rows_out[pl.ds(pl.multiple_of(a * 16, 16), 16), :] = acc.astype(BF16)
        return 0

    lax.fori_loop(0, 16, block_row, 0, unroll=True)
    pick = one_hot(iota((256, 32), 0) == 8 * iota((256, 32), 1))
    lat[...] = jnp.dot(rows_out[...], pick, preferred_element_type=F32).astype(BF16)
    px, tok = iota((256, 128), 0), iota((256, 128), 1)
    for w in range(2):
        acc = jnp.zeros((32, 128), F32)
        for r in range(8):
            place = one_hot((px == 16 * (tok & 15) + 8 * w) & ((tok >> 4) == r))
            acc = acc + jnp.dot(
                rows_out[32 * r : 32 * r + 32], place, preferred_element_type=F32
            )
        t = level[0]
        mixed = (1.0 - t) * acc + t * noise[32 * w : 32 * w + 32].astype(F32)
        pat[32 * w : 32 * w + 32] = mixed.astype(BF16)


def attend_body(pats, parts, gram, att):
    tokens_t = jnp.concatenate([pats[s] for s in range(4)], axis=1).astype(F32)
    tokens = tokens_t.T
    spread = jnp.sum(
        tokens
        * jnp.dot(
            tokens, gram[...], precision=lax.Precision.HIGHEST, preferred_element_type=F32
        ),
        axis=1,
        keepdims=True,
    )
    scale = lax.rsqrt(spread + 1e-06)
    total = parts[0].astype(F32)
    for i in range(1, 16):
        total = total + parts[i].astype(F32)
    hi = total.astype(BF16)
    lo = (total - hi.astype(F32)).astype(BF16)
    weights = jnp.concatenate([hi, lo], axis=0)
    twice = jnp.concatenate([tokens, tokens], axis=1).astype(BF16)
    for h in range(3):
        proj = jnp.dot(
            twice, weights[:, 384 * h : 384 * h + 384], preferred_element_type=F32
        )
        proj = (proj * scale).astype(BF16)
        q, k, v = proj[:, 0:128], proj[:, 128:256], proj[:, 256:384]
        scores = lax.dot_general(
            q, k, (((1,), (1,)), ((), ())), preferred_element_type=F32
        ) * (1.0 / math.sqrt(128.0))
        probs = jnp.exp(scores - jnp.max(scores, axis=1, keepdims=True))
        norm = 1.0 / jnp.sum(probs, axis=1, keepdims=True)
        out = jnp.dot(probs.astype(BF16), v, preferred_element_type=F32) * norm
        att[:, 128 * h : 128 * h + 128] = out.astype(BF16)


def grad_body(place, att, c0, c_up, c_down, far_a, far_b, out, full, blocks):
    sec, y, core = place[0], place[1], place[2]
    sides = []
    for step in (0, 3, 1, 2):
        row = pl.multiple_of(((sec + step) & 3) * 128, 128)
        sides.append(att[pl.ds(row, 128), :])
    rhs = jnp.concatenate(sides, axis=0)
    for half, far in enumerate((far_a, far_b)):
        rows = slice(768 * half, 768 * half + 768)
        lhs = jnp.concatenate([c0[rows], c_up[rows], c_down[rows], far[...]], axis=1)
        full[rows] = jnp.dot(lhs, rhs, preferred_element_type=F32)
    for to_core in range(2):
        for to_y in range(4):
            slot = ((to_core + core) & 1) * 4 + ((to_y - y) & 3)
            for zx in range(16):
                first = 12 * (8 * zx + 2 * to_y + to_core)
                blocks[slot, 12 * zx : 12 * zx + 12] = full[first : first + 12]
    for slot in range(8):
        out[slot] = blocks[slot].astype(BF16)


def pack_body(cot, bottom, top, up, down):
    up[0:1536] = cot[...]
    down[0:1536] = cot[...]
    up[1536:1552] = bottom[...]
    down[1536:1552] = top[...]


def together(*values):
    return lax.optimization_barrier(values)


def moved(shard, axis, size, by, wrap):
    pairs = [(i, (i + by) % size) for i in range(size) if wrap or 0 <= i + by < size]
    return lax.ppermute(shard, axis, pairs)


def on_device(
    video,
    conv_weight,
    down_weight,
    noise,
    timesteps,
    embed_weight,
    mod_weight,
    qkv_weight,
    cotangent,
):
    rims = [
        jnp.pad(video[:, 0, row].reshape(6, 128), ((0, 10), (0, 0))) for row in (127, 0)
    ]
    cot, cot_top = call(
        pack_body, [jax.ShapeDtypeStruct((1552, 128), BF16)] * 2, 0, 3, 0, 10**6
    )(cotangent[0].T, *rims)
    c_up = moved(cot, "sec", 4, 1, True)
    c_down = moved(cot_top, "sec", 4, -1, True)

    rows = lax.all_to_all(
        jnp.broadcast_to(qkv_weight.transpose(1, 0, 2), (8, 3, 24, 384)), ("zl", "core"), 0, 0, tiled=True
    )
    rows = rows.transpose(1, 0, 2, 3).reshape(3, 192, 384)
    stamps = lax.all_gather(timesteps, ("x", "y"), axis=0, tiled=True)

    frequency = jnp.exp(-math.log(10000.0) * jnp.arange(128, dtype=F32) / 128)
    angles = stamps.astype(F32)[:, None] * frequency[None, :]
    temb = jnp.concatenate([jnp.cos(angles), jnp.sin(angles)], axis=1)
    place = (lax.axis_index("x") * 4 + lax.axis_index("y")).astype(jnp.int32)[None]
    a_hi, a_lo, gram = call(
        prep_body,
        [
            jax.ShapeDtypeStruct((1024, 192), BF16),
            jax.ShapeDtypeStruct((1024, 192), BF16),
            jax.ShapeDtypeStruct((64, 64), F32),
        ],
        1,
        3,
        10**9,
        3 * 10**6,
    )(place, embed_weight, mod_weight, temb)
    partial = call(
        fold_body, jax.ShapeDtypeStruct((1024, 1152), BF16), 0, 3, 10**9, 5 * 10**6
    )(a_hi, a_lo, rows)
    partial, c_up, c_down = together(partial, c_up, c_down)
    sec = lax.axis_index("sec").astype(jnp.int32)[None]
    above = jnp.where(sec[0] == 0, 0, c_up[1536:1542]).astype(BF16).reshape(3, 1, 1, 256)
    below = jnp.where(sec[0] == 3, 0, c_down[1536:1542]).astype(BF16).reshape(3, 1, 1, 256)
    v0 = jnp.concatenate([video, above, below], axis=2)
    v1, v2 = moved(v0, SEQ, 128, 1, False), moved(v0, SEQ, 128, 2, False)
    partial, v1, v2 = together(partial, v1, v2)

    taps = conv_weight.reshape(128, 3, 3, 3, 3).transpose(0, 3, 4, 1, 2).reshape(128, 3, 27)
    taps = jnp.pad(taps, ((0, 0), (0, 0), (0, 5))).reshape(128, 96)
    conv = jnp.concatenate(
        [jnp.pad(taps, ((0, 0), (0, 32))), jnp.pad(taps, ((0, 0), (32, 0)))], axis=0
    )
    down = down_weight.transpose(1, 2, 3, 0).reshape(8, 128, 128)
    noise_t = noise.reshape(16, 8, 2, 16, 2).transpose(4, 2, 0, 1, 3).reshape(64, 128)
    level = (timesteps.astype(F32) + 1.0) / STEPS
    lat, pat = call(
        encode_body,
        [jax.ShapeDtypeStruct((256, 32), BF16), jax.ShapeDtypeStruct((64, 128), BF16)],
        1,
        6,
        10**10,
        10**6,
        [
            pltpu.VMEM((32, 128, 256), F32),
            pltpu.VMEM((64, 256), F32),
            pltpu.VMEM((4160, 256), BF16),
            pltpu.VMEM((256, 256), BF16),
        ],
    )(level, v2, v1, v0, conv, down, noise_t)
    latents = lat.reshape(16, 16, 32).transpose(1, 0, 2)[:, None]

    far_a = moved(c_up[0:768], "sec", 4, 1, True)
    far_b = moved(c_down[768:1536], "sec", 4, -1, True)
    pat, far_a, far_b = together(pat, far_a, far_b)
    parts = lax.all_to_all(partial.reshape(16, 64, 1152), ("x", "y"), 0, 0, tiled=True)
    pats = lax.all_gather(pat, "sec", axis=0)
    att = call(
        attend_body, jax.ShapeDtypeStruct((512, 384), BF16), 0, 3, 4 * 10**9, 10**6
    )(pats, parts, gram)
    attended = lax.all_to_all(att, "sec", split_axis=0, concat_axis=1, tiled=True)

    blocks = call(
        grad_body,
        jax.ShapeDtypeStruct((8, 192, 384), BF16),
        1,
        6,
        10**9,
        5 * 10**6,
        [pltpu.VMEM((1536, 384), F32), pltpu.VMEM((8, 192, 384), F32)],
    )(
        jnp.stack([sec[0], lax.axis_index("y"), lax.axis_index("core")]).astype(jnp.int32),
        att,
        cot,
        c_up,
        c_down,
        far_a,
        far_b,
    )
    other = moved(blocks[4:8], "core", 2, 1, True)
    pair_sum = (blocks[0:4].astype(F32) + other.astype(F32)).astype(BF16)
    got = [moved(pair_sum[by], "y", 4, by, True) for by in range(1, 4)]
    row_sum = sum([g.astype(F32) for g in got], pair_sum[0].astype(F32)).astype(BF16)
    last = lax.all_to_all(row_sum.reshape(16, 12, 384), ("zl", "x"), 0, 0, tiled=True)
    out_grad = jnp.sum(last.astype(F32), axis=0)
    return (latents, attended[None], out_grad)


def solution(mesh):
    split = Mesh(mesh.devices.reshape(4, 4, 4, 4, 2), ("sec",) + SEQ)
    in_specs = (
        P(None, SEQ, "sec", None),
        P(),
        P(),
        P(None, SEQ, "sec", None),
        P(SEQ),
        P(),
        P(),
        P(SEQ, "sec", None),
        P(SEQ, "sec", None),
    )
    out_specs = (P(None, SEQ, "sec", None), P(SEQ, "sec", None), P(SEQ, "sec"))
    return jax.shard_map(
        on_device, mesh=split, in_specs=in_specs, out_specs=out_specs, check_vma=False
    )
```

```python
import math

import jax
import jax.numpy as jnp
from jax import lax
from jax.experimental import pallas as pl
from jax.experimental.pallas import tpu as pltpu
from jax.sharding import Mesh, PartitionSpec as P

STEPS = 1000
SEQ = ("zl", "x", "y", "core")
F32 = jnp.float32
BF16 = jnp.bfloat16
VMEM = pl.BlockSpec(memory_space=pltpu.VMEM)
SMEM = pl.BlockSpec(memory_space=pltpu.SMEM)
ANY = pl.BlockSpec(memory_space=pl.ANY)
VMEM_BYTES = 48 * 1024 * 1024


def call(body, out_shape, n_smem, n_vmem, flops, nbytes, scratch=(), n_any=0):
    several = isinstance(out_shape, (list, tuple))
    return pl.pallas_call(
        body,
        out_shape=out_shape,
        in_specs=[SMEM] * n_smem + [VMEM] * n_vmem + [ANY] * n_any,
        out_specs=[VMEM] * len(out_shape) if several else VMEM,
        scratch_shapes=list(scratch),
        compiler_params=pltpu.CompilerParams(vmem_limit_bytes=VMEM_BYTES),
        cost_estimate=pl.CostEstimate(flops=flops // 10**6, bytes_accessed=nbytes // 10**5, transcendentals=0),
    )


def iota(shape, dim):
    return lax.broadcasted_iota(jnp.int32, shape, dim)


def one_hot(where):
    return jnp.where(where, 1.0, 0.0).astype(BF16)


def prep_body(place, embed, mod, temb, a_hi, a_lo, gram):
    to, of = iota((64, 64), 0), iota((64, 64), 1)
    order = one_hot(of == (to & 15) * 4 + ((to >> 4) & 1) * 2 + (to >> 5))
    emb = jnp.dot(order, embed[...], preferred_element_type=F32)
    mean = jnp.mean(emb, axis=1, keepdims=True)
    center = emb - mean
    gram[...] = (
        lax.dot_general(
            center,
            center,
            (((1,), (1,)), ((), ())),
            precision=lax.Precision.HIGHEST,
            preferred_element_type=F32,
        )
        / embed.shape[1]
    )
    col = iota((768, 192), 1)
    part = (col * 1366) >> 16
    hit = iota((768, 192), 0) == 48 * place[0] + col - 48 * part
    emb16 = emb.astype(BF16)
    emb_pick = jnp.zeros((64, 192), F32)
    mod_pick = jnp.zeros((256, 192), F32)
    for z in range(4):
        pick = one_hot(hit & (part == z))
        at = slice(768 * z, 768 * z + 768)
        emb_pick = emb_pick + jnp.dot(emb16[:, at], pick, preferred_element_type=F32)
        mod_pick = mod_pick + jnp.dot(mod[:, at], pick, preferred_element_type=F32)
    emb_pick = emb_pick - mean
    t = temb[...]
    first = t.astype(BF16).astype(F32)
    second = (t - first).astype(BF16).astype(F32)
    third = t - first - second
    pieces = jnp.concatenate([first, second, third], axis=0).astype(BF16)
    scale = jnp.dot(pieces, mod_pick.astype(BF16), preferred_element_type=F32)
    scale = 1.0 + (scale[0:16] + scale[16:32] + scale[32:48])
    for f in range(16):
        a = emb_pick * scale[f : f + 1]
        hi = a.astype(BF16)
        a_hi[64 * f : 64 * f + 64] = hi
        a_lo[64 * f : 64 * f + 64] = (a - hi.astype(F32)).astype(BF16)


def fold_body(a_hi, a_lo, w, noise, conv, out):
    for h in range(3):
        prod = jnp.dot(a_hi[...], w[h], preferred_element_type=F32) + jnp.dot(
            a_lo[...], w[h], preferred_element_type=F32
        )
        out[:, 384 * h : 384 * h + 384] = prod.astype(BF16)


def encode_body(
    level, v2, v1, v0, conv, down, noise, lat, pat, s32, edge, s16, rows_out
):
    x = iota((136, 256), 1)
    for c in range(3):
        for dt, v in enumerate((v2, v1, v0)):
            img = v[c, 0].astype(F32)
            left = jnp.where(x[:130] == 0, 0.0, pltpu.roll(img, 1, 1))
            right = jnp.where(x[:130] == 255, 0.0, pltpu.roll(img, 255, 1))
            for dx, shifted in enumerate((left, img, right)):
                k = dx * 9 + c * 3 + dt
                s32[k] = shifted[0:128]
                edge[k : k + 1] = shifted[128:129]
                edge[32 + k : 33 + k] = shifted[129:130]
    s32[27:32] = jnp.zeros((5, 128, 256), F32)
    edge[27:32] = jnp.zeros((5, 256), F32)
    edge[59:64] = jnp.zeros((5, 256), F32)
    s16[0:32] = edge[0:32].astype(BF16)
    s16[4128:4160] = edge[32:64].astype(BF16)
    for y in range(0, 128, 8):
        taps = jnp.swapaxes(s32[:, y : y + 8, :], 0, 1).reshape(256, 256)
        s16[32 * y + 32 : 32 * y + 288] = taps.astype(BF16)
    own_lane = (iota((128, 256), 1) & 7) == (iota((128, 256), 0) >> 4)

    def block_row(a, _):
        feats = []
        for q in range(4):
            taps = s16[pl.ds(pl.multiple_of(a * 256 + 64 * q, 64), 128), :]
            pre = jnp.dot(conv[...], taps, preferred_element_type=F32)
            half = 0.5 * pre
            feats.append((half + half * jnp.tanh(half)).astype(BF16))
        feature = jnp.concatenate(feats, axis=0)
        weights = jnp.concatenate([down[i] for i in range(8)], axis=1)
        prod = jnp.dot(weights, feature, preferred_element_type=F32)
        prod = jnp.where(own_lane, prod, 0.0)
        acc = prod[0:16]
        for j in range(1, 8):
            acc = acc + prod[16 * j : 16 * j + 16]
        for by in (1, 2, 4):
            acc = acc + pltpu.roll(acc, 256 - by, 1)
        rows_out[pl.ds(pl.multiple_of(a * 16, 16), 16), :] = acc.astype(BF16)
        return 0

    lax.fori_loop(0, 16, block_row, 0, unroll=True)
    pick = one_hot(iota((256, 32), 0) == 8 * iota((256, 32), 1))
    lat[...] = jnp.dot(rows_out[...], pick, preferred_element_type=F32).astype(BF16)
    px, tok = iota((256, 128), 0), iota((256, 128), 1)
    for w in range(2):
        acc = jnp.zeros((32, 128), F32)
        for r in range(8):
            place = one_hot((px == 16 * (tok & 15) + 8 * w) & ((tok >> 4) == r))
            acc = acc + jnp.dot(
                rows_out[32 * r : 32 * r + 32], place, preferred_element_type=F32
            )
        t = level[0]
        mixed = (1.0 - t) * acc + t * noise[32 * w : 32 * w + 32].astype(F32)
        pat[32 * w : 32 * w + 32] = mixed.astype(BF16)


def attend_body(pats, parts, gram, att):
    tokens_t = jnp.concatenate([pats[s] for s in range(4)], axis=1).astype(F32)
    tokens = tokens_t.T
    spread = jnp.sum(
        tokens
        * jnp.dot(
            tokens, gram[...], precision=lax.Precision.HIGHEST, preferred_element_type=F32
        ),
        axis=1,
        keepdims=True,
    )
    scale = lax.rsqrt(spread + 1e-06)
    total = parts[0].astype(F32)
    for i in range(1, 16):
        total = total + parts[i].astype(F32)
    hi = total.astype(BF16)
    lo = (total - hi.astype(F32)).astype(BF16)
    weights = jnp.concatenate([hi, lo], axis=0)
    twice = jnp.concatenate([tokens, tokens], axis=1).astype(BF16)
    for h in range(3):
        proj = jnp.dot(
            twice, weights[:, 384 * h : 384 * h + 384], preferred_element_type=F32
        )
        proj = (proj * scale).astype(BF16)
        q, k, v = proj[:, 0:128], proj[:, 128:256], proj[:, 256:384]
        scores = lax.dot_general(
            q, k, (((1,), (1,)), ((), ())), preferred_element_type=F32
        ) * (1.0 / math.sqrt(128.0))
        probs = jnp.exp(scores - jnp.max(scores, axis=1, keepdims=True))
        norm = 1.0 / jnp.sum(probs, axis=1, keepdims=True)
        out = jnp.dot(probs.astype(BF16), v, preferred_element_type=F32) * norm
        att[:, 128 * h : 128 * h + 128] = out.astype(BF16)


def grad_body(place, att, c0, c_up, c_down, far_a, far_b, out, full, blocks):
    sec, y, core = place[0], place[1], place[2]
    sides = []
    for step in (0, 3, 1, 2):
        row = pl.multiple_of(((sec + step) & 3) * 128, 128)
        sides.append(att[pl.ds(row, 128), :])
    rhs = jnp.concatenate(sides, axis=0)
    for half, far in enumerate((far_a, far_b)):
        rows = slice(768 * half, 768 * half + 768)
        lhs = jnp.concatenate([c0[rows], c_up[rows], c_down[rows], far[...]], axis=1)
        full[rows] = jnp.dot(lhs, rhs, preferred_element_type=F32)
    for to_core in range(2):
        for to_y in range(4):
            slot = ((to_core + core) & 1) * 4 + ((to_y - y) & 3)
            for zx in range(16):
                first = 12 * (8 * zx + 2 * to_y + to_core)
                blocks[slot, 12 * zx : 12 * zx + 12] = full[first : first + 12]
    for slot in range(8):
        out[slot] = blocks[slot].astype(BF16)


def pack_body(cot, bottom, top, up, down):
    up[0:1536] = cot[...]
    down[0:1536] = cot[...]
    up[1536:1552] = bottom[...]
    down[1536:1552] = top[...]


def together(*values):
    return lax.optimization_barrier(values)


def moved(shard, axis, size, by, wrap):
    pairs = [(i, (i + by) % size) for i in range(size) if wrap or 0 <= i + by < size]
    return lax.ppermute(shard, axis, pairs)


def on_device(
    video,
    conv_weight,
    down_weight,
    noise,
    timesteps,
    embed_weight,
    mod_weight,
    qkv_weight,
    cotangent,
):
    rims = [
        jnp.pad(video[:, 0, row].reshape(6, 128), ((0, 10), (0, 0))) for row in (127, 0)
    ]
    cot, cot_top = call(
        pack_body, [jax.ShapeDtypeStruct((1552, 128), BF16)] * 2, 0, 3, 0, 10**6
    )(cotangent[0].T, *rims)
    c_up = moved(cot, "sec", 4, 1, True)
    c_down = moved(cot_top, "sec", 4, -1, True)

    rows = lax.all_to_all(
        jnp.broadcast_to(qkv_weight.transpose(1, 0, 2), (8, 3, 24, 384)), ("zl", "core"), 0, 0, tiled=True
    )
    rows = rows.transpose(1, 0, 2, 3).reshape(3, 192, 384)
    stamps = lax.all_gather(timesteps, ("x", "y"), axis=0, tiled=True)

    frequency = jnp.exp(-math.log(10000.0) * jnp.arange(128, dtype=F32) / 128)
    angles = stamps.astype(F32)[:, None] * frequency[None, :]
    temb = jnp.concatenate([jnp.cos(angles), jnp.sin(angles)], axis=1)
    place = (lax.axis_index("x") * 4 + lax.axis_index("y")).astype(jnp.int32)[None]
    a_hi, a_lo, gram = call(
        prep_body,
        [
            jax.ShapeDtypeStruct((1024, 192), BF16),
            jax.ShapeDtypeStruct((1024, 192), BF16),
            jax.ShapeDtypeStruct((64, 64), F32),
        ],
        1,
        3,
        10**9,
        3 * 10**6,
    )(place, embed_weight, mod_weight, temb)
    taps = conv_weight.reshape(128, 3, 3, 3, 3).transpose(0, 3, 4, 1, 2).reshape(128, 3, 27)
    taps = jnp.pad(taps, ((0, 0), (0, 0), (0, 5))).reshape(128, 96)
    conv = jnp.concatenate(
        [jnp.pad(taps, ((0, 0), (0, 32))), jnp.pad(taps, ((0, 0), (32, 0)))], axis=0
    )
    noise_t = noise.reshape(16, 8, 2, 16, 2).transpose(4, 2, 0, 1, 3).reshape(64, 128)
    partial = call(
        fold_body, jax.ShapeDtypeStruct((1024, 1152), BF16), 0, 3, 10**9, 5 * 10**6, (), 2
    )(a_hi, a_lo, rows, noise_t, conv)
    partial, c_up, c_down = together(partial, c_up, c_down)
    sec = lax.axis_index("sec").astype(jnp.int32)[None]
    above = jnp.where(sec[0] == 0, 0, c_up[1536:1542]).astype(BF16).reshape(3, 1, 1, 256)
    below = jnp.where(sec[0] == 3, 0, c_down[1536:1542]).astype(BF16).reshape(3, 1, 1, 256)
    v0 = jnp.concatenate([video, above, below], axis=2)
    v1, v2 = moved(v0, SEQ, 128, 1, False), moved(v0, SEQ, 128, 2, False)
    partial, v1, v2 = together(partial, v1, v2)

    down = down_weight.transpose(1, 2, 3, 0).reshape(8, 128, 128)
    level = (timesteps.astype(F32) + 1.0) / STEPS
    lat, pat = call(
        encode_body,
        [jax.ShapeDtypeStruct((256, 32), BF16), jax.ShapeDtypeStruct((64, 128), BF16)],
        1,
        6,
        10**10,
        10**6,
        [
            pltpu.VMEM((32, 128, 256), F32),
            pltpu.VMEM((64, 256), F32),
            pltpu.VMEM((4160, 256), BF16),
            pltpu.VMEM((256, 256), BF16),
        ],
    )(level, v2, v1, v0, conv, down, noise_t)
    latents = lat.reshape(16, 16, 32).transpose(1, 0, 2)[:, None]

    far_a = moved(c_up[0:768], "sec", 4, 1, True)
    far_b = moved(c_down[768:1536], "sec", 4, -1, True)
    pat, far_a, far_b = together(pat, far_a, far_b)
    parts = lax.all_to_all(partial.reshape(16, 64, 1152), ("x", "y"), 0, 0, tiled=True)
    pats = lax.all_gather(pat, "sec", axis=0)
    att = call(
        attend_body, jax.ShapeDtypeStruct((512, 384), BF16), 0, 3, 4 * 10**9, 10**6
    )(pats, parts, gram)
    attended = lax.all_to_all(att, "sec", split_axis=0, concat_axis=1, tiled=True)

    blocks = call(
        grad_body,
        jax.ShapeDtypeStruct((8, 192, 384), BF16),
        1,
        6,
        10**9,
        5 * 10**6,
        [pltpu.VMEM((1536, 384), F32), pltpu.VMEM((8, 192, 384), F32)],
    )(
        jnp.stack([sec[0], lax.axis_index("y"), lax.axis_index("core")]).astype(jnp.int32),
        att,
        cot,
        c_up,
        c_down,
        far_a,
        far_b,
    )
    other = moved(blocks[4:8], "core", 2, 1, True)
    pair_sum = (blocks[0:4].astype(F32) + other.astype(F32)).astype(BF16)
    got = [moved(pair_sum[by], "y", 4, by, True) for by in range(1, 4)]
    row_sum = sum([g.astype(F32) for g in got], pair_sum[0].astype(F32)).astype(BF16)
    last = lax.all_to_all(row_sum.reshape(16, 12, 384), ("zl", "x"), 0, 0, tiled=True)
    out_grad = jnp.sum(last.astype(F32), axis=0)
    return (latents, attended[None], out_grad)


def solution(mesh):
    split = Mesh(mesh.devices.reshape(4, 4, 4, 4, 2), ("sec",) + SEQ)
    in_specs = (
        P(None, SEQ, "sec", None),
        P(),
        P(),
        P(None, SEQ, "sec", None),
        P(SEQ),
        P(),
        P(),
        P(SEQ, "sec", None),
        P(SEQ, "sec", None),
    )
    out_specs = (P(None, SEQ, "sec", None), P(SEQ, "sec", None), P(SEQ, "sec"))
    return jax.shard_map(
        on_device, mesh=split, in_specs=in_specs, out_specs=out_specs, check_vma=False
    )
```
